512 devices in a mesh: member: 8 (over y, core), dp: 4 (over x), block: 16 (over z).
Axes of the slice: x: 4, y: 4, z: 16, core: 2. Of those that a mesh axis runs over, the one named last changes fastest.
Arguments:
- a_train: bfloat16 [16384, 1024], P(('member', 'block'), 'dp'), parts along dimension 0, may hold values from -6 to 6
- g_train: bfloat16 [32768, 1024], P(('member', 'block'), 'dp'), parts along dimension 0, may hold values from -6 to 6
- a_query: bfloat16 [16384, 128], P(('member', 'block')), parts along dimension 0, may hold values from -6 to 6
- g_query: bfloat16 [32768, 128], P(('member', 'block')), parts along dimension 0, may hold values from -6 to 6
- basis_in: bfloat16 [16384, 2048], P('member', 'block'), parts along dimension 0, may hold values from -0.125 to 0.125
- basis_out: bfloat16 [32768, 4096], P('member', 'block'), parts along dimension 0, may hold values from -0.09375 to 0.09375
- eigen: float32 [16384, 4096], P(('member', 'block'), 'dp'), parts along dimension 0, may hold values from 0.05 to 5
Outputs:
- influence: float32 [64, 64], P('member', 'dp'), parts along dimension 0
The draws below stay inside these ranges and needn't reach their ends.
There are 8 independent parts, one for each index of `member`. The reference program is written for one: setup_inputs(seed, part) draws one part's arguments, and reference() takes and returns one part's arrays. A program takes and returns all parts, laid end to end along the dimension named above; each array names one. Nothing has to cross between parts.
All inputs are finite; a program needn't handle non-finite values.
Results may differ from the reference program's by a relative error of at most 0.0052.
Values may be sent and summed in bfloat16 or wider, within the bound.
A program may use at most 64 MiB of HBM per device.

```python
import math
import jax
import jax.numpy as jnp
from jax import lax

DIN = 2048
DOUT = 4096
STEPS = 16
NQ = 8
QSTEPS = 16
EPISODES = 64


def steps_of(rng, shape, pieces, smallest, top_value):
    def one(axis_at, blocks):
        heights = jax.random.uniform(jax.random.fold_in(jax.random.fold_in(rng, 6), axis_at), (blocks,), jnp.float32, smallest / len(pieces), top_value / len(pieces))
        return jnp.repeat(jnp.exp(heights), shape[axis_at] // blocks).reshape((-1,) + (1,) * (len(shape) - axis_at - 1))

    factor_of = one(*pieces[0])
    for cut in pieces[1:]:
        factor_of = factor_of * one(*cut)
    return factor_of


def bell_draw(stream_key, dims, deviation, most, split=(), kind=jnp.bfloat16):
    drawn = jax.random.normal(stream_key, dims, jnp.float32) * deviation
    if len(split) > 0:
        drawn = steps_of(stream_key, dims, split, -0.22, 0.18) * drawn
    return jnp.clip(drawn, min=-most, max=most).astype(kind)


def setup_inputs(seed: int = 0, part: int = 0) -> dict:
    key_list = jax.random.split(jax.random.key(seed), 8)
    part_keys = jax.random.split(jax.random.fold_in(key_list[7], part), 8)
    a_train = bell_draw(part_keys[0], (DIN, EPISODES * STEPS), 1.0, 6.0, ((0, 16), (1, 4)))
    g_train = bell_draw(part_keys[1], (DOUT, EPISODES * STEPS), 1.0, 6.0, ((0, 16), (1, 4)))
    a_query = bell_draw(part_keys[2], (DIN, NQ * QSTEPS), 1.0, 6.0, ((0, 16),))
    g_query = bell_draw(part_keys[3], (DOUT, NQ * QSTEPS), 1.0, 6.0, ((0, 16),))
    basis_in = bell_draw(part_keys[4], (DIN, DIN), DIN ** -0.5, 0.125, ((1, 16),))
    basis_out = bell_draw(part_keys[5], (DOUT, DOUT), DOUT ** -0.5, 0.09375, ((1, 16),))
    eigen = jnp.clip(jnp.exp(math.log(5.0) - 4.6051702 * jax.random.uniform(part_keys[6], (DIN, DOUT), jnp.float32) ** steps_of(part_keys[6], (DIN, DOUT), ((0, 16), (1, 4)), -0.2, 0.2)), 0.05, 5.0)
    return {"a_train": a_train, "g_train": g_train, "a_query": a_query, "g_query": g_query, "basis_in": basis_in, "basis_out": basis_out, "eigen": eigen}


damping = 0.05

def reference(a_train, g_train, a_query, g_query, basis_in, basis_out, eigen):
    rot_at = jnp.dot(basis_in.T, a_train, preferred_element_type=jnp.float32).astype(jnp.bfloat16)
    rot_aq = jnp.dot(basis_in.T, a_query, preferred_element_type=jnp.float32).astype(jnp.bfloat16)
    rot_gt = jnp.dot(basis_out.T, g_train, preferred_element_type=jnp.float32).astype(jnp.bfloat16)
    rot_gq = jnp.dot(basis_out.T, g_query, preferred_element_type=jnp.float32).astype(jnp.bfloat16)
    damped = eigen + damping
    query_a = rot_aq.reshape(DIN, NQ, QSTEPS).transpose(1, 0, 2)
    query_g = rot_gq.reshape(DOUT, NQ, QSTEPS).transpose(1, 0, 2)
    train_af = rot_at.astype(jnp.float32)

    def one_query(pair):
        part_a, part_g = pair
        query_grad = jnp.dot(part_a, part_g.T, preferred_element_type=jnp.float32)
        precond = (query_grad / damped).astype(jnp.bfloat16)
        norm_value = jnp.sum(query_grad * query_grad / damped)
        inner = jnp.dot(precond, rot_gt, preferred_element_type=jnp.float32)
        column_score = lax.optimization_barrier(jnp.sum(inner * train_af, axis=0))
        episode_score = column_score.reshape(EPISODES, STEPS).sum(axis=1)
        return episode_score / jnp.sqrt(norm_value * STEPS)
    return lax.map(one_query, (query_a, query_g))
```

```python
import functools

import jax
import jax.numpy as jnp
from jax import lax
from jax.experimental import pallas as pl
from jax.experimental.pallas import tpu as pltpu
from jax.sharding import PartitionSpec as P

STEPS = 16
NQ = 8
QSTEPS = 16
DAMPING = 0.05

MESH = pl.DeviceIdType.MESH
BF16 = jnp.bfloat16
F32 = jnp.float32


def contract_rows(left, right):
    return lax.dot_general(left, right, (((0,), (0,)), ((), ())), preferred_element_type=F32)


def kernel(
    nz, nx,
    a_ref, g_ref, aq_ref, gq_ref, bi_ref, bo_ref, eig_ref,
    out_ref,
    g_buf, a_buf, gq_buf, aq_buf, rg_buf, rgq_buf, bo, bi, eig, inv,
    g_acc, a_acc, gq_part, gq_recv, aq_part, aq_recv, aq_mask, x_acc, norm_acc, msg, sums,
    ring_send, ring_recv, x_send, x_recv, xg_send, xg_recv, z_send, z_recv, local_sem,
):
    half = nz // 2
    me = lax.axis_index("block")
    dp = lax.axis_index("dp")
    n_in, n_t = a_ref.shape
    n_out = g_ref.shape[0]
    n_c = aq_ref.shape[1]
    q_in, q_out = n_in // nx, n_out // nx
    per_dp = nz // nx

    def z_peer(k):
        return {"block": lax.rem(me + (k + nz), nz)}

    def x_peer(k):
        return {"dp": lax.rem(dp + k, nx)}

    def source(slot):
        return lax.rem(me + nz - slot, nz)

    locals_ = [
        pltpu.make_async_copy(eig_ref, eig, local_sem.at[0]),
        pltpu.make_async_copy(bo_ref, bo, local_sem.at[1]),
        pltpu.make_async_copy(g_ref, g_buf.at[0], local_sem.at[2]),
        pltpu.make_async_copy(bi_ref, bi, local_sem.at[3]),
        pltpu.make_async_copy(a_ref, a_buf.at[0], local_sem.at[4]),
        pltpu.make_async_copy(gq_ref.at[pl.ds(pl.multiple_of(dp * q_out, q_out), q_out)], gq_buf.at[0], local_sem.at[5]),
        pltpu.make_async_copy(aq_ref.at[pl.ds(pl.multiple_of(dp * q_in, q_in), q_in)], aq_buf.at[0], local_sem.at[6]),
    ]
    for copy in locals_:
        copy.start()

    barrier = pltpu.get_barrier_semaphore()
    for k in range(1, nz):
        pl.semaphore_signal(barrier, inc=1, device_id=z_peer(k), device_id_type=MESH)
    for k in range(1, nx):
        pl.semaphore_signal(barrier, inc=1, device_id=x_peer(k), device_id_type=MESH)

    def ring(index, buf, first, rows):
        start, size = rows
        start = start if isinstance(start, int) else pl.multiple_of(start, size)

        def at(ref, lo, n):
            return ref.at[pl.ds(start + lo, n)]

        def copy(way, hop, part):
            lo, n = (0, size) if not part else ((0, size // 2) if way == 0 else (size // 2, size // 2))
            own = isinstance(hop, int) and hop == 0
            src_slot, dst_slot = (hop, hop + 1) if way == 0 else (lax.rem(nz - hop, nz), nz - 1 - hop)
            src = at(first, lo, n) if own else at(buf.at[src_slot], lo, n)
            return pltpu.make_async_remote_copy(
                src_ref=src, dst_ref=at(buf.at[dst_slot], lo, n),
                send_sem=ring_send.at[index, way, hop], recv_sem=ring_recv.at[index, way, hop],
                device_id=z_peer(1 if way == 0 else -1), device_id_type=MESH,
            )

        def begin():
            for way in (0, 1):
                copy(way, 0, False).start()

        def step(hop):
            last = isinstance(hop, int) and hop == half
            for way in (0, 1):
                copy(way, hop - 1, last).wait_recv()
                if not last:
                    copy(way, hop, isinstance(hop, int) and hop == half - 1).start()

        def finish():
            for way in (0, 1):
                def body(hop, c):
                    copy(way, hop, False).wait_send()
                    return c
                copy(way, 0, False).wait_send()
                lax.fori_loop(1, half - 1, body, 0)
                copy(way, half - 1, True).wait_send()

        return begin, step, finish

    ho, hi = n_out // 2, n_in // 2
    gq_ring = ring(0, gq_buf, gq_buf.at[0], (0, q_out))
    g0_ring = ring(1, g_buf, g_ref, (0, ho))
    g1_ring = ring(2, g_buf, g_ref, (ho, ho))
    aq_ring = ring(3, aq_buf, aq_buf.at[0], (0, q_in))
    a0_ring = ring(4, a_buf, a_ref, (0, hi))
    a1_ring = ring(5, a_buf, a_ref, (hi, hi))
    rg0_ring = ring(6, rg_buf, rg_buf.at[0], (0, ho))
    rg1_ring = ring(7, rg_buf, rg_buf.at[0], (ho, ho))
    rgq_ring = ring(8, rgq_buf, rgq_buf.at[0], (dp * q_out, q_out))

    locals_[5].wait()
    locals_[6].wait()
    pl.semaphore_wait(barrier, nz - 1 + nx - 1)

    for one in (gq_ring, g0_ring, g1_ring, aq_ring, a0_ring):
        one[0]()

    locals_[0].wait()
    for k in range(per_dp):
        inv[dp * per_dp + k] = 1.0 / (eig[:, k * n_out:(k + 1) * n_out] + DAMPING)

    def inv_copy(k):
        mine = inv.at[pl.ds(dp * per_dp, per_dp)]
        return pltpu.make_async_remote_copy(
            src_ref=mine, dst_ref=mine, send_sem=x_send.at[0, k - 1], recv_sem=x_recv.at[0, k - 1],
            device_id=x_peer(k), device_id_type=MESH,
        )

    def inv_arrival(k):
        theirs = inv.at[pl.ds(lax.rem(dp + nx - k, nx) * per_dp, per_dp)]
        return pltpu.make_async_remote_copy(
            src_ref=theirs, dst_ref=theirs, send_sem=x_send.at[0, k - 1], recv_sem=x_recv.at[0, k - 1],
            device_id=x_peer(k), device_id_type=MESH,
        )

    for k in range(1, nx):
        inv_copy(k).start()

    def rotate_g(slot):
        rows = pl.ds(pl.multiple_of(source(slot) * n_out, n_out), n_out)
        return contract_rows(bo[rows, :], g_buf[slot])

    def rotate_a(slot):
        rows = pl.ds(pl.multiple_of(source(slot) * n_in, n_in), n_in)
        return contract_rows(bi[rows, :], a_buf[slot])

    for k in (1, 2, 3, 4):
        locals_[k].wait()
    g_acc[...] = rotate_g(0)
    x_acc[...] = jnp.zeros_like(x_acc)
    norm_acc[...] = jnp.zeros_like(norm_acc)

    def first(hop):
        gq_ring[1](hop)
        g0_ring[1](hop)
        g1_ring[1](hop)
        aq_ring[1](hop)

    def first_body(hop, c):
        first(hop)
        a0_ring[1](hop)
        g_acc[...] += rotate_g(hop) + rotate_g(nz - hop)
        return c

    lax.fori_loop(1, half - 1, first_body, 0)
    first(half - 1)
    a0_ring[1](half - 1)
    a1_ring[0]()
    g_acc[...] += rotate_g(half - 1) + rotate_g(half + 1)
    g0_ring[1](half)
    g1_ring[1](half)
    rg_buf[0] = (g_acc[...] + rotate_g(half)).astype(BF16)
    rg0_ring[0]()
    rg1_ring[0]()

    gq_ring[1](half)

    def stack(ref, width, n):
        pieces = []
        for slot in range(nz):
            at = pl.multiple_of(source(slot) * width + dp * n, n)
            pieces.append(ref[pl.ds(at, n), :])
        return jnp.concatenate(pieces, axis=0)

    gq_part[...] = contract_rows(stack(bo, n_out, q_out), gq_buf[...].reshape(nz * q_out, n_c))

    def gq_copy(k):
        rows = pl.ds(pl.multiple_of(lax.rem(dp + k, nx) * q_out, q_out), q_out)
        return pltpu.make_async_remote_copy(
            src_ref=gq_part.at[rows], dst_ref=gq_recv.at[k - 1],
            send_sem=x_send.at[1, k - 1], recv_sem=x_recv.at[1, k - 1], device_id=x_peer(k), device_id_type=MESH,
        )

    def aq_copy(k):
        return pltpu.make_async_remote_copy(
            src_ref=aq_part, dst_ref=aq_recv.at[k - 1],
            send_sem=x_send.at[2, k - 1], recv_sem=x_recv.at[2, k - 1], device_id=x_peer(k), device_id_type=MESH,
        )

    for k in range(1, nx):
        gq_copy(k).start()
    aq_ring[1](half)
    aq_part[...] = contract_rows(stack(bi, n_in, q_in), aq_buf[...].reshape(nz * q_in, n_c))
    for k in range(1, nx):
        aq_copy(k).start()
    a0_ring[1](half)
    a_acc[...] = rotate_a(0)

    my_rows = pl.ds(pl.multiple_of(dp * q_out, q_out), q_out)

    def rgq_copy(slot, k):
        mine = rgq_buf.at[slot, my_rows]
        return pltpu.make_async_remote_copy(
            src_ref=mine, dst_ref=mine, send_sem=xg_send.at[slot, k - 1], recv_sem=xg_recv.at[slot, k - 1],
            device_id=x_peer(k), device_id_type=MESH,
        )

    def rgq_arrival(slot, k):
        rows = pl.ds(pl.multiple_of(lax.rem(dp + nx - k, nx) * q_out, q_out), q_out)
        theirs = rgq_buf.at[slot, rows]
        return pltpu.make_async_remote_copy(
            src_ref=theirs, dst_ref=theirs, send_sem=xg_send.at[slot, k - 1], recv_sem=xg_recv.at[slot, k - 1],
            device_id=x_peer(k), device_id_type=MESH,
        )

    for k in range(1, nx):
        gq_copy(k).wait_recv()
    rgq_buf[0, my_rows] = (gq_part[my_rows] + gq_recv[0] + gq_recv[1] + gq_recv[2]).astype(BF16)
    rgq_ring[0]()
    for k in range(1, nx):
        rgq_copy(0, k).start()
    for k in range(1, nx):
        aq_copy(k).wait_recv()
    rot_aq = (aq_part[...] + aq_recv[0] + aq_recv[1] + aq_recv[2]).astype(BF16)
    column = lax.broadcasted_iota(jnp.int32, (n_in, n_c), 1)
    for q in range(NQ):
        aq_mask[q * n_in:(q + 1) * n_in, :] = jnp.where(column // QSTEPS == q, rot_aq.astype(F32), 0.0).astype(BF16)
    for k in range(1, nx):
        inv_arrival(k).wait_recv()

    group = 2

    def score_block(slot):
        block_inv = inv[source(slot)]
        queries = rgq_buf[slot]
        train = rg_buf[slot]
        for part in range(NQ // group):
            rows = pl.ds(part * group * n_in, group * n_in)
            grad = lax.dot_general(
                aq_mask[rows, :], queries, (((1,), (1,)), ((), ())), preferred_element_type=F32
            ).reshape(group, n_in, n_out)
            precond = grad * block_inv[None]
            terms = (grad * precond).reshape(group, n_in // 8, 8, n_out).sum(axis=1)
            for lane in range(n_out // 128):
                norm_acc[part * group:(part + 1) * group] += terms[:, :, lane * 128:(lane + 1) * 128]
            x_acc[rows, :] += jnp.dot(
                precond.astype(BF16).reshape(group * n_in, n_out), train, preferred_element_type=F32
            )

    def gather_sends(slot):
        for k in range(1, nx):
            rgq_copy(slot, k).start()

    def gather_waits(slot):
        for k in range(1, nx):
            rgq_arrival(slot, k).wait_recv()

    def second(hop):
        rg0_ring[1](hop)
        rg1_ring[1](hop)
        a1_ring[1](hop)

    second(1)
    a_acc[...] += rotate_a(1) + rotate_a(nz - 1)
    gather_waits(0)
    score_block(0)

    second(2)
    rgq_ring[1](1)
    gather_sends(1)
    gather_sends(nz - 1)
    a_acc[...] += rotate_a(2) + rotate_a(nz - 2)

    def second_body(hop, c):
        second(hop)
        rgq_ring[1](hop - 1)
        gather_sends(hop - 1)
        gather_sends(nz - hop + 1)
        a_acc[...] += rotate_a(hop) + rotate_a(nz - hop)
        gather_waits(hop - 2)
        score_block(hop - 2)
        gather_waits(nz - hop + 2)
        score_block(nz - hop + 2)
        return c

    lax.fori_loop(3, half - 1, second_body, 0)
    second(half - 1)
    rgq_ring[1](half - 2)
    gather_sends(half - 2)
    gather_sends(half + 2)
    a_acc[...] += rotate_a(half - 1) + rotate_a(half + 1)

    def late_body(slot, c):
        gather_waits(slot)
        score_block(slot)
        return c

    for slot in (half - 3, half + 3):
        late_body(slot, 0)
    rgq_ring[1](half - 1)
    gather_sends(half - 1)
    gather_sends(half + 1)
    for slot in (half - 2, half + 2):
        late_body(slot, 0)
    rgq_ring[1](half)
    gather_sends(half)
    second(half)
    a_acc[...] += rotate_a(half)
    lax.fori_loop(half - 1, half + 2, late_body, 0)

    rot_a = a_acc[...].astype(BF16).astype(F32)
    for q in range(NQ):
        msg_row = jnp.sum(x_acc[q * n_in:(q + 1) * n_in, :] * rot_a, axis=0, keepdims=True)
        g_acc[q:q + 1, :] = msg_row
    step_of = lax.broadcasted_iota(jnp.int32, (n_t, 128), 0) // STEPS
    episode = lax.broadcasted_iota(jnp.int32, (n_t, 128), 1)
    pick = jnp.where(step_of == episode, 1.0, 0.0)
    scores = jnp.dot(
        g_acc[0:NQ, :], pick, preferred_element_type=F32, precision=lax.Precision.HIGHEST
    )
    norms = jnp.sum(jnp.sum(norm_acc[...], axis=1), axis=1, keepdims=True)
    lanes = lax.broadcasted_iota(jnp.int32, (NQ, 128), 1)
    msg[...] = jnp.where(lanes == 127, norms, scores)

    def sum_copy(k):
        return pltpu.make_async_remote_copy(
            src_ref=msg, dst_ref=sums.at[k - 1], send_sem=z_send.at[k - 1], recv_sem=z_recv.at[k - 1],
            device_id=z_peer(k), device_id_type=MESH,
        )

    for k in range(1, nz):
        sum_copy(k).start()

    for one in (gq_ring, g0_ring, g1_ring, aq_ring, a0_ring, a1_ring, rg0_ring, rg1_ring, rgq_ring):
        one[2]()
    for k in range(1, nx):
        inv_copy(k).wait_send()
        gq_copy(k).wait_send()
        aq_copy(k).wait_send()

    def sent_body(slot, c):
        for k in range(1, nx):
            rgq_copy(slot, k).wait_send()
        return c

    lax.fori_loop(0, nz, sent_body, 0)
    total = msg[...]
    for k in range(1, nz):
        sum_copy(k).wait_recv()
        total += sums[k - 1]
    for k in range(1, nz):
        sum_copy(k).wait_send()
    out_ref[...] = total


def shards(nz, nx, a_train, g_train, a_query, g_query, basis_in, basis_out, eigen):
    n_in, n_t = a_train.shape
    n_out = g_train.shape[0]
    n_c = a_query.shape[1]
    q_in, q_out = n_in // nx, n_out // nx
    vmem = pltpu.VMEM
    dma = pltpu.SemaphoreType.DMA
    total = pl.pallas_call(
        functools.partial(kernel, nz, nx),
        out_shape=jax.ShapeDtypeStruct((NQ, 128), F32),
        in_specs=[pl.BlockSpec(memory_space=pl.ANY)] * 7,
        out_specs=pl.BlockSpec(memory_space=vmem),
        scratch_shapes=[
            vmem((nz, n_out, n_t), BF16),
            vmem((nz, n_in, n_t), BF16),
            vmem((nz, q_out, n_c), BF16),
            vmem((nz, q_in, n_c), BF16),
            vmem((nz, n_out, n_t), BF16),
            vmem((nz, n_out, n_c), BF16),
            vmem(basis_out.shape, BF16),
            vmem(basis_in.shape, BF16),
            vmem(eigen.shape, F32),
            vmem((nz, n_in, n_out), F32),
            vmem((n_out, n_t), F32),
            vmem((n_in, n_t), F32),
            vmem((n_out, n_c), F32),
            vmem((nx - 1, q_out, n_c), F32),
            vmem((n_in, n_c), F32),
            vmem((nx - 1, n_in, n_c), F32),
            vmem((NQ * n_in, n_c), BF16),
            vmem((NQ * n_in, n_t), F32),
            vmem((NQ, 8, 128), F32),
            vmem((NQ, 128), F32),
            vmem((nz - 1, NQ, 128), F32),
            dma((9, 2, nz // 2)),
            dma((9, 2, nz // 2)),
            dma((3, nx - 1)),
            dma((3, nx - 1)),
            dma((nz, nx - 1)),
            dma((nz, nx - 1)),
            dma((nz - 1,)),
            dma((nz - 1,)),
            dma((7,)),
        ],
        compiler_params=pltpu.CompilerParams(
            collective_id=0, has_side_effects=True, vmem_limit_bytes=48 * 2**20
        ),
    )(a_train, g_train, a_query, g_query, basis_in, basis_out, eigen)
    return total[:, : n_t // STEPS] / jnp.sqrt(total[:, 127:128] * STEPS)


def solution(mesh):
    in_specs = (
        P(("member", "block"), "dp"),
        P(("member", "block"), "dp"),
        P(("member", "block"), None),
        P(("member", "block"), None),
        P("member", "block"),
        P("member", "block"),
        P(("member", "block"), "dp"),
    )
    body = functools.partial(shards, mesh.shape["block"], mesh.shape["dp"])
    return jax.shard_map(body, mesh=mesh, in_specs=in_specs, out_specs=P("member", "dp"), check_vma=False)
```

```python
import functools

import jax
import jax.numpy as jnp
from jax import lax
from jax.experimental import pallas as pl
from jax.experimental.pallas import tpu as pltpu
from jax.sharding import PartitionSpec as P

STEPS = 16
NQ = 8
QSTEPS = 16
DAMPING = 0.05

MESH = pl.DeviceIdType.MESH
BF16 = jnp.bfloat16
F32 = jnp.float32


def contract_rows(left, right):
    return lax.dot_general(left, right, (((0,), (0,)), ((), ())), preferred_element_type=F32)


def kernel(
    nz, nx, a_lead,
    a_ref, g_ref, aq_ref, gq_ref, bi_ref, bo_ref, eig_ref,
    out_ref,
    g_buf, a_buf, gq_buf, aq_buf, rg_buf, rgq_buf, bo, bi, eig, inv,
    g_acc, a_acc, gq_part, gq_recv, aq_part, aq_recv, aq_mask, x_acc, norm_acc, msg, sums,
    ring_send, ring_recv, x_send, x_recv, xg_send, xg_recv, z_send, z_recv, local_sem,
):
    half = nz // 2
    stages = half // 2
    me = lax.axis_index("block")
    dp = lax.axis_index("dp")
    n_in, n_t = a_ref.shape
    n_out = g_ref.shape[0]
    n_c = aq_ref.shape[1]
    q_in, q_out = n_in // nx, n_out // nx
    per_dp = nz // nx
    my_rows = pl.ds(pl.multiple_of(dp * q_out, q_out), q_out)

    def z_peer(k):
        return {"block": lax.rem(me + (k + nz), nz)}

    def x_peer(k):
        return {"dp": lax.rem(dp + k, nx)}

    def source(slot):
        return lax.rem(me + nz - slot, nz)

    locals_ = [
        pltpu.make_async_copy(gq_ref.at[my_rows], gq_buf.at[0], local_sem.at[0]),
        pltpu.make_async_copy(aq_ref.at[pl.ds(pl.multiple_of(dp * q_in, q_in), q_in)], aq_buf.at[0], local_sem.at[1]),
        pltpu.make_async_copy(eig_ref, eig, local_sem.at[2]),
        pltpu.make_async_copy(g_ref, g_buf.at[0], local_sem.at[3]),
        pltpu.make_async_copy(bo_ref, bo, local_sem.at[4]),
        pltpu.make_async_copy(a_ref, a_buf.at[0], local_sem.at[5]),
        pltpu.make_async_copy(bi_ref, bi, local_sem.at[6]),
    ]
    for copy in locals_:
        copy.start()

    barrier = pltpu.get_barrier_semaphore()
    near = (1, 2, -1, -2)
    for k in near:
        pl.semaphore_signal(barrier, inc=1, device_id=z_peer(k), device_id_type=MESH)
    for k in range(1, nx):
        pl.semaphore_signal(barrier, inc=1, device_id=x_peer(k), device_id_type=MESH)

    def remote(src, dst, send_sem, recv_sem, device):
        return pltpu.make_async_remote_copy(
            src_ref=src, dst_ref=dst, send_sem=send_sem, recv_sem=recv_sem,
            device_id=device, device_id_type=MESH,
        )

    def extent(way, part, lo, size):
        if not part:
            return pl.ds(lo, size)
        return pl.ds(lo + way * (size // 2), size // 2)

    class Ring:
        def __init__(self, index, buf, first, lo, size):
            self.index, self.buf, self.first, self.lo, self.size = index, buf, first, lo, size

        def copy(self, way, hop, part, own=False):
            rows = extent(way, part, self.lo, self.size)
            src_slot, dst_slot = (hop, hop + 1) if way == 0 else (lax.rem(nz - hop, nz), nz - 1 - hop)
            src = self.first.at[rows] if own else self.buf.at[src_slot, rows]
            return remote(
                src, self.buf.at[dst_slot, rows], ring_send.at[self.index, way, hop],
                ring_recv.at[self.index, way, hop], z_peer(1 if way == 0 else -1),
            )

        def begin(self):
            for way in (0, 1):
                self.copy(way, 0, False, own=True).start()

        def relay(self, hop):
            for way in (0, 1):
                self.copy(way, hop - 1, False).wait_recv()
                self.copy(way, hop, False).start()

        def relay_last(self):
            for way in (0, 1):
                self.copy(way, half - 2, False).wait_recv()
                self.copy(way, half - 1, True).start()

        def end(self):
            for way in (0, 1):
                self.copy(way, half - 1, True).wait_recv()

        def at(self, hop):
            pl.when(hop < half - 1)(lambda: self.relay(hop))
            pl.when(hop == half - 1)(self.relay_last)
            pl.when(hop == half)(self.end)

        def sent(self):
            def body(hop, c):
                for way in (0, 1):
                    self.copy(way, hop, False).wait_send()
                return c

            lax.fori_loop(0, half - 1, body, 0)
            for way in (0, 1):
                self.copy(way, half - 1, True).wait_send()

    class Stride:
        def __init__(self, index, buf, lo, size):
            self.index, self.buf, self.lo, self.size = index, buf, lo, size

        def copy(self, way, stage, ahead, part=False):
            rows = extent(way, part, self.lo, self.size)
            base = 2 * (stage - 1)
            src_slot, dst_slot = (base, base + ahead) if way == 0 else (lax.rem(nz - base, nz), nz - base - ahead)
            sem = base + ahead - 1
            return remote(
                self.buf.at[src_slot, rows], self.buf.at[dst_slot, rows], ring_send.at[self.index, way, sem],
                ring_recv.at[self.index, way, sem], z_peer(ahead if way == 0 else -ahead),
            )

        def send(self, stage, last=False):
            for way in (0, 1):
                self.copy(way, stage, 2, last).start()
            for way in (0, 1):
                self.copy(way, stage, 1).start()

        def take(self, stage, last=False):
            for way in (0, 1):
                self.copy(way, stage, 2, last).wait_recv()
            for way in (0, 1):
                self.copy(way, stage, 1).wait_recv()

        def relay(self, stage, last):
            for way in (0, 1):
                self.copy(way, stage, 2).wait_recv()
                self.copy(way, stage + 1, 2, last).start()
                self.copy(way, stage + 1, 1).start()
            for way in (0, 1):
                self.copy(way, stage, 1).wait_recv()

        def sent(self):
            for stage in range(1, stages + 1):
                for way in (0, 1):
                    self.copy(way, stage, 2, stage == stages).wait_send()
                    self.copy(way, stage, 1).wait_send()

    ho = n_out // 2
    gq_ring = Stride(0, gq_buf, 0, q_out)
    aq_ring = Stride(1, aq_buf, 0, q_in)
    rgq_ring = Stride(2, rgq_buf, pl.multiple_of(dp * q_out, q_out), q_out)
    g_rings = (Ring(3, g_buf, g_ref, 0, ho), Ring(4, g_buf, g_ref, ho, ho))
    rg_rings = (Ring(5, rg_buf, rg_buf.at[0], 0, ho), Ring(6, rg_buf, rg_buf.at[0], ho, ho))
    a_ring = Ring(7, a_buf, a_ref, 0, n_in)

    locals_[0].wait()
    locals_[1].wait()
    pl.semaphore_wait(barrier, len(near) + nx - 1)

    gq_ring.send(1)
    for ring in g_rings:
        ring.begin()
    aq_ring.send(1)

    locals_[2].wait()
    for k in range(per_dp):
        inv[dp * per_dp + k] = 1.0 / (eig[:, k * n_out:(k + 1) * n_out] + DAMPING)

    def inv_copy(k, hop):
        owner = lax.rem(dp + nx - k * hop, nx)
        if hop == 0:
            rows = pl.ds(owner * per_dp, per_dp)
        else:
            rows = pl.ds(owner * per_dp + (0 if k == 1 else per_dp // 2), per_dp // 2)
        sem = 2 * hop + (0 if k == 1 else 1)
        return remote(inv.at[rows], inv.at[rows], x_send.at[0, sem], x_recv.at[0, sem], x_peer(lax.rem(k + nx, nx)))

    def inv_send(hop):
        for k in (1, -1):
            inv_copy(k, hop).start()

    def inv_take(hop):
        for k in (1, -1):
            owner = lax.rem(dp + nx - k * (hop + 1), nx)
            if hop == 0:
                rows = pl.ds(owner * per_dp, per_dp)
            else:
                rows = pl.ds(owner * per_dp + (0 if k == 1 else per_dp // 2), per_dp // 2)
            sem = 2 * hop + (0 if k == 1 else 1)
            remote(
                inv.at[rows], inv.at[rows], x_send.at[0, sem], x_recv.at[0, sem], x_peer(lax.rem(k + nx, nx))
            ).wait_recv()

    inv_send(0)

    def rotate_g(slot):
        rows = pl.ds(pl.multiple_of(source(slot) * n_out, n_out), n_out)
        return contract_rows(bo[rows, :], g_buf[slot])

    def rotate_a(slot):
        rows = pl.ds(pl.multiple_of(source(slot) * n_in, n_in), n_in)
        return contract_rows(bi[rows, :], a_buf[slot])

    for copy in locals_[3:]:
        copy.wait()
    g_acc[...] = rotate_g(0)
    a_acc[...] = rotate_a(0)
    x_acc[...] = jnp.zeros_like(x_acc)
    norm_acc[...] = jnp.zeros_like(norm_acc)

    def stack(ref, width, n):
        pieces = []
        for slot in range(nz):
            at = pl.multiple_of(source(slot) * width + dp * n, n)
            pieces.append(ref[pl.ds(at, n), :])
        return jnp.concatenate(pieces, axis=0)

    def gq_copy(k):
        rows = pl.ds(pl.multiple_of(lax.rem(dp + k, nx) * q_out, q_out), q_out)
        return remote(gq_part.at[rows], gq_recv.at[k - 1], x_send.at[1, k - 1], x_recv.at[1, k - 1], x_peer(k))

    def aq_copy(k):
        return remote(aq_part, aq_recv.at[k - 1], x_send.at[2, k - 1], x_recv.at[2, k - 1], x_peer(k))

    def query_sums():
        gq_ring.take(stages, True)
        gq_part[...] = contract_rows(stack(bo, n_out, q_out), gq_buf[...].reshape(nz * q_out, n_c))
        for k in range(1, nx):
            gq_copy(k).start()
        aq_ring.take(stages, True)
        aq_part[...] = contract_rows(stack(bi, n_in, q_in), aq_buf[...].reshape(nz * q_in, n_c))
        for k in range(1, nx):
            aq_copy(k).start()

    def rgq_copy(first, n, k, theirs=False):
        rows = pl.ds(pl.multiple_of(lax.rem(dp + nx - k, nx) * q_out, q_out), q_out) if theirs else my_rows
        ref = rgq_buf.at[pl.ds(first, n), rows]
        return remote(ref, ref, xg_send.at[first, k - 1], xg_recv.at[first, k - 1], x_peer(k))

    def gather_groups(stage):
        if isinstance(stage, int) and stage == 0:
            return ((0, 1),)
        if isinstance(stage, int) and stage == stages:
            return ((2 * stage - 1, 3),)
        return ((2 * stage - 1, 2), (nz - 2 * stage, 2))

    def gather(stage):
        for first, n in gather_groups(stage):
            for k in range(1, nx):
                rgq_copy(first, n, k).start()

    def gathered(stage):
        for first, n in gather_groups(stage):
            for k in range(1, nx):
                rgq_copy(first, n, k, theirs=True).wait_recv()

    def query_rotations():
        for k in range(1, nx):
            gq_copy(k).wait_recv()
        rgq_buf[0, my_rows] = (gq_part[my_rows] + gq_recv[0] + gq_recv[1] + gq_recv[2]).astype(BF16)
        rgq_ring.send(1)
        gather(0)
        for k in range(1, nx):
            aq_copy(k).wait_recv()
        rot_aq = (aq_part[...] + aq_recv[0] + aq_recv[1] + aq_recv[2]).astype(BF16).astype(F32)
        column = lax.broadcasted_iota(jnp.int32, (n_in, n_c), 1)
        for q in range(NQ):
            aq_mask[q * n_in:(q + 1) * n_in, :] = jnp.where(column // QSTEPS == q, rot_aq, 0.0).astype(BF16)

    def first_body(hop, c):
        @pl.when(hop < stages - 1)
        def _():
            gq_ring.relay(hop, False)

        @pl.when(hop == stages - 1)
        def _():
            gq_ring.relay(stages - 1, True)

        for ring in g_rings:
            ring.at(hop)

        @pl.when(hop < stages - 1)
        def _():
            aq_ring.relay(hop, False)

        @pl.when(hop == stages - 1)
        def _():
            aq_ring.relay(stages - 1, True)
            inv_take(0)
            inv_send(1)

        pl.when(hop == stages)(query_sums)
        pl.when(hop == stages + 1)(query_rotations)

        @pl.when(hop == stages + 2)
        def _():
            rgq_ring.relay(1, False)
            gather(1)

        @pl.when(hop == stages + 3)
        def _():
            rgq_ring.relay(2, False)
            gather(2)

        pl.when(hop == a_lead)(a_ring.begin)
        pl.when(hop > a_lead)(lambda: a_ring.relay(hop - a_lead))

        g_acc[...] += rotate_g(hop) + rotate_g(nz - hop)
        return c

    lax.fori_loop(1, half, first_body, 0)
    for ring in g_rings:
        ring.end()
    rg_buf[0] = (g_acc[...] + rotate_g(half)).astype(BF16)
    for ring in rg_rings:
        ring.begin()
    rgq_ring.relay(stages - 1, True)
    gather(stages - 1)
    a_ring.relay(half - a_lead)
    inv_take(1)
    gathered(0)

    group = 2

    def score_block(slot):
        block_inv = inv[source(slot)]
        queries = rgq_buf[slot]
        train = rg_buf[slot]
        for part in range(NQ // group):
            rows = pl.ds(part * group * n_in, group * n_in)
            grad = lax.dot_general(
                aq_mask[rows, :], queries, (((1,), (1,)), ((), ())), preferred_element_type=F32
            ).reshape(group, n_in, n_out)
            precond = grad * block_inv[None]
            terms = (grad * precond).reshape(group, n_in // 8, 8, n_out).sum(axis=1)
            for lane in range(n_out // 128):
                norm_acc[part * group:(part + 1) * group] += terms[:, :, lane * 128:(lane + 1) * 128]
            x_acc[rows, :] += jnp.dot(
                precond.astype(BF16).reshape(group * n_in, n_out), train, preferred_element_type=F32
            )

    def second_body(hop, c):
        for ring in rg_rings:
            ring.at(hop)

        @pl.when(hop == 1)
        def _():
            rgq_ring.take(stages, True)
            gather(stages)

        pl.when(hop + half - a_lead <= half)(lambda: a_ring.at(hop + half - a_lead))

        @pl.when(lax.rem(hop, 2) == 1)
        def _():
            stage = (hop + 1) // 2
            pl.when(stage < stages)(lambda: gathered(stage))
            pl.when(stage == stages)(lambda: gathered(stages))

        pl.when(hop == 1)(lambda: score_block(0))

        def blocks(i, c):
            slot = jnp.where(i == 0, hop, nz - hop)
            score_block(slot)
            a_acc[...] += rotate_a(slot)
            return c

        lax.fori_loop(0, jnp.where(hop == half, 1, 2), blocks, 0)
        return c

    lax.fori_loop(1, half + 1, second_body, 0)

    rot_a = a_acc[...].astype(BF16).astype(F32)
    for q in range(NQ):
        g_acc[q:q + 1, :] = jnp.sum(x_acc[q * n_in:(q + 1) * n_in, :] * rot_a, axis=0, keepdims=True)
    step_of = lax.broadcasted_iota(jnp.int32, (n_t, 128), 0) // STEPS
    episode = lax.broadcasted_iota(jnp.int32, (n_t, 128), 1)
    pick = jnp.where(step_of == episode, 1.0, 0.0)
    scores = jnp.dot(
        g_acc[0:NQ, :], pick, preferred_element_type=F32, precision=lax.Precision.HIGHEST
    )
    norms = jnp.sum(jnp.sum(norm_acc[...], axis=1), axis=1, keepdims=True)
    lanes = lax.broadcasted_iota(jnp.int32, (NQ, 128), 1)
    msg[...] = jnp.where(lanes == 127, norms, scores)

    def sum_copy(k):
        return remote(msg, sums.at[k - 1], z_send.at[k - 1], z_recv.at[k - 1], z_peer(k))

    order = sorted(range(1, nz), key=lambda k: -min(k, nz - k))
    for k in order:
        sum_copy(k).start()

    for ring in (gq_ring, aq_ring, rgq_ring) + g_rings + rg_rings + (a_ring,):
        ring.sent()
    for hop in (0, 1):
        for k in (1, -1):
            inv_copy(k, hop).wait_send()
    for k in range(1, nx):
        gq_copy(k).wait_send()
        aq_copy(k).wait_send()
    for stage in range(stages + 1):
        for start, n in gather_groups(stage):
            for k in range(1, nx):
                rgq_copy(start, n, k).wait_send()

    total = msg[...]
    for k in range(1, nz):
        sum_copy(k).wait_recv()
        total += sums[k - 1]
    out_ref[...] = (total / jnp.sqrt(total[:, 127:128] * QSTEPS))[:, : out_ref.shape[1]]
    for k in range(1, nz):
        sum_copy(k).wait_send()


def shards(nz, nx, a_train, g_train, a_query, g_query, basis_in, basis_out, eigen):
    n_in, n_t = a_train.shape
    n_out = g_train.shape[0]
    n_c = a_query.shape[1]
    q_in, q_out = n_in // nx, n_out // nx
    vmem = pltpu.VMEM
    dma = pltpu.SemaphoreType.DMA
    return pl.pallas_call(
        functools.partial(kernel, nz, nx, nz // 2 - 2),
        out_shape=jax.ShapeDtypeStruct((NQ, n_t // STEPS), F32),
        in_specs=[pl.BlockSpec(memory_space=pl.ANY)] * 7,
        out_specs=pl.BlockSpec(memory_space=vmem),
        scratch_shapes=[
            vmem((nz, n_out, n_t), BF16),
            vmem((nz, n_in, n_t), BF16),
            vmem((nz, q_out, n_c), BF16),
            vmem((nz, q_in, n_c), BF16),
            vmem((nz, n_out, n_t), BF16),
            vmem((nz, n_out, n_c), BF16),
            vmem(basis_out.shape, BF16),
            vmem(basis_in.shape, BF16),
            vmem(eigen.shape, F32),
            vmem((nz, n_in, n_out), F32),
            vmem((n_out, n_t), F32),
            vmem((n_in, n_t), F32),
            vmem((n_out, n_c), F32),
            vmem((nx - 1, q_out, n_c), F32),
            vmem((n_in, n_c), F32),
            vmem((nx - 1, n_in, n_c), F32),
            vmem((NQ * n_in, n_c), BF16),
            vmem((NQ * n_in, n_t), F32),
            vmem((NQ, 8, 128), F32),
            vmem((NQ, 128), F32),
            vmem((nz - 1, NQ, 128), F32),
            dma((8, 2, nz // 2)),
            dma((8, 2, nz // 2)),
            dma((3, 4)),
            dma((3, 4)),
            dma((nz, nx - 1)),
            dma((nz, nx - 1)),
            dma((nz - 1,)),
            dma((nz - 1,)),
            dma((7,)),
        ],
        compiler_params=pltpu.CompilerParams(
            collective_id=0, has_side_effects=True, vmem_limit_bytes=56 * 2**20
        ),
    )(a_train, g_train, a_query, g_query, basis_in, basis_out, eigen)


def solution(mesh):
    in_specs = (
        P(("member", "block"), "dp"),
        P(("member", "block"), "dp"),
        P(("member", "block"), None),
        P(("member", "block"), None),
        P("member", "block"),
        P("member", "block"),
        P(("member", "block"), "dp"),
    )
    body = functools.partial(shards, mesh.shape["block"], mesh.shape["dp"])
    return jax.shard_map(body, mesh=mesh, in_specs=in_specs, out_specs=P("member", "dp"), check_vma=False)
```

```python
import functools

import jax
import jax.numpy as jnp
from jax import lax
from jax.experimental import pallas as pl
from jax.experimental.pallas import tpu as pltpu
from jax.sharding import PartitionSpec as P

STEPS = 16
NQ = 8
QSTEPS = 16
DAMPING = 0.05

A_LEAD = 6
Q_SUM = 4
Q_ROT = 6
G_CUTS = 4
A_CUTS = 2

MESH = pl.DeviceIdType.MESH
BF16 = jnp.bfloat16
F32 = jnp.float32


def contract_rows(left, right):
    return lax.dot_general(left, right, (((0,), (0,)), ((), ())), preferred_element_type=F32)


def kernel(
    nz, nx, g_cuts, a_cuts,
    a_ref, g_ref, aq_ref, gq_ref, bi_ref, bo_ref, eig_ref,
    out_ref,
    g_buf, a_buf, gq_buf, aq_buf, rg_buf, rgq_buf, bo, bi, eig, inv,
    g_acc, a_acc, gq_part, gq_recv, aq_part, aq_recv, aq_mask, x_acc, norm_acc, msg, sums,
    ring_send, ring_recv, x_send, x_recv, xg_send, xg_recv, z_send, z_recv, local_sem,
):
    half = nz // 2
    stages = half // 2
    me = lax.axis_index("block")
    dp = lax.axis_index("dp")
    n_in, n_t = a_ref.shape
    n_out = g_ref.shape[0]
    n_c = aq_ref.shape[1]
    q_in, q_out = n_in // nx, n_out // nx
    per_dp = nz // nx
    my_rows = pl.ds(pl.multiple_of(dp * q_out, q_out), q_out)

    def z_peer(k):
        return {"block": lax.rem(me + (k + nz), nz)}

    def x_peer(k):
        return {"dp": lax.rem(dp + k, nx)}

    def source(slot):
        return lax.rem(me + nz - slot, nz)

    locals_ = [
        pltpu.make_async_copy(gq_ref.at[my_rows], gq_buf.at[0], local_sem.at[0]),
        pltpu.make_async_copy(aq_ref.at[pl.ds(pl.multiple_of(dp * q_in, q_in), q_in)], aq_buf.at[0], local_sem.at[1]),
        pltpu.make_async_copy(eig_ref, eig, local_sem.at[2]),
        pltpu.make_async_copy(g_ref, g_buf.at[0], local_sem.at[3]),
        pltpu.make_async_copy(bo_ref, bo, local_sem.at[4]),
        pltpu.make_async_copy(a_ref, a_buf.at[0], local_sem.at[5]),
        pltpu.make_async_copy(bi_ref, bi, local_sem.at[6]),
    ]
    for copy in locals_:
        copy.start()

    barrier = pltpu.get_barrier_semaphore()
    near = (1, 2, -1, -2)
    for k in near:
        pl.semaphore_signal(barrier, inc=1, device_id=z_peer(k), device_id_type=MESH)
    for k in range(1, nx):
        pl.semaphore_signal(barrier, inc=1, device_id=x_peer(k), device_id_type=MESH)

    def remote(src, dst, send_sem, recv_sem, device):
        return pltpu.make_async_remote_copy(
            src_ref=src, dst_ref=dst, send_sem=send_sem, recv_sem=recv_sem,
            device_id=device, device_id_type=MESH,
        )

    def extent(way, part, lo, size):
        if not part:
            return pl.ds(lo, size)
        return pl.ds(lo + way * (size // 2), size // 2)

    class Ring:
        def __init__(self, index, buf, first, lo, size):
            self.index, self.buf, self.first, self.lo, self.size = index, buf, first, lo, size

        def copy(self, way, hop, part, own=False):
            rows = extent(way, part, self.lo, self.size)
            src_slot, dst_slot = (hop, hop + 1) if way == 0 else (lax.rem(nz - hop, nz), nz - 1 - hop)
            src = self.first.at[rows] if own else self.buf.at[src_slot, rows]
            return remote(
                src, self.buf.at[dst_slot, rows], ring_send.at[self.index, way, hop],
                ring_recv.at[self.index, way, hop], z_peer(1 if way == 0 else -1),
            )

        def begin(self):
            for way in (0, 1):
                self.copy(way, 0, False, own=True).start()

        def relay(self, hop):
            for way in (0, 1):
                self.copy(way, hop - 1, False).wait_recv()
                self.copy(way, hop, False).start()

        def relay_last(self):
            for way in (0, 1):
                self.copy(way, half - 2, False).wait_recv()
                self.copy(way, half - 1, True).start()

        def end(self):
            for way in (0, 1):
                self.copy(way, half - 1, True).wait_recv()

        def at(self, hop):
            pl.when(hop < half - 1)(lambda: self.relay(hop))
            pl.when(hop == half - 1)(self.relay_last)
            pl.when(hop == half)(self.end)

        def sent(self):
            def body(hop, c):
                for way in (0, 1):
                    self.copy(way, hop, False).wait_send()
                return c

            lax.fori_loop(0, half - 1, body, 0)
            for way in (0, 1):
                self.copy(way, half - 1, True).wait_send()

    class Stride:
        def __init__(self, index, buf, lo, size):
            self.index, self.buf, self.lo, self.size = index, buf, lo, size

        def copy(self, way, stage, ahead, part=False):
            rows = extent(way, part, self.lo, self.size)
            base = 2 * (stage - 1)
            src_slot, dst_slot = (base, base + ahead) if way == 0 else (lax.rem(nz - base, nz), nz - base - ahead)
            sem = base + ahead - 1
            return remote(
                self.buf.at[src_slot, rows], self.buf.at[dst_slot, rows], ring_send.at[self.index, way, sem],
                ring_recv.at[self.index, way, sem], z_peer(ahead if way == 0 else -ahead),
            )

        def send(self, stage, last=False):
            for way in (0, 1):
                self.copy(way, stage, 2, last).start()
            for way in (0, 1):
                self.copy(way, stage, 1).start()

        def take(self, stage, last=False):
            for way in (0, 1):
                self.copy(way, stage, 2, last).wait_recv()
            for way in (0, 1):
                self.copy(way, stage, 1).wait_recv()

        def relay(self, stage, last):
            for way in (0, 1):
                self.copy(way, stage, 2).wait_recv()
                self.copy(way, stage + 1, 2, last).start()
                self.copy(way, stage + 1, 1).start()
            for way in (0, 1):
                self.copy(way, stage, 1).wait_recv()

        def sent(self):
            for stage in range(1, stages + 1):
                for way in (0, 1):
                    self.copy(way, stage, 2, stage == stages).wait_send()
                    self.copy(way, stage, 1).wait_send()

    ho, hi = n_out // g_cuts, n_in // a_cuts
    gq_ring = Stride(0, gq_buf, 0, q_out)
    aq_ring = Ring(1, aq_buf, aq_buf.at[0], 0, q_in)
    rgq_ring = Ring(2, rgq_buf, rgq_buf.at[0], pl.multiple_of(dp * q_out, q_out), q_out)
    g_rings = tuple(Ring(3 + c, g_buf, g_ref, c * ho, ho) for c in range(g_cuts))
    rg_rings = tuple(Ring(3 + g_cuts + c, rg_buf, rg_buf.at[0], c * ho, ho) for c in range(g_cuts))
    a_rings = tuple(Ring(3 + 2 * g_cuts + c, a_buf, a_ref, c * hi, hi) for c in range(a_cuts))

    locals_[0].wait()
    locals_[1].wait()
    pl.semaphore_wait(barrier, len(near) + nx - 1)

    gq_ring.send(1)
    for ring in g_rings:
        ring.begin()
    aq_ring.begin()

    locals_[2].wait()
    for k in range(per_dp):
        inv[dp * per_dp + k] = 1.0 / (eig[:, k * n_out:(k + 1) * n_out] + DAMPING)

    def inv_copy(k, hop):
        owner = lax.rem(dp + nx - k * hop, nx)
        if hop == 0:
            rows = pl.ds(owner * per_dp, per_dp)
        else:
            rows = pl.ds(owner * per_dp + (0 if k == 1 else per_dp // 2), per_dp // 2)
        sem = 2 * hop + (0 if k == 1 else 1)
        return remote(inv.at[rows], inv.at[rows], x_send.at[0, sem], x_recv.at[0, sem], x_peer(lax.rem(k + nx, nx)))

    def inv_send(hop):
        for k in (1, -1):
            inv_copy(k, hop).start()

    def inv_take(hop):
        for k in (1, -1):
            owner = lax.rem(dp + nx - k * (hop + 1), nx)
            if hop == 0:
                rows = pl.ds(owner * per_dp, per_dp)
            else:
                rows = pl.ds(owner * per_dp + (0 if k == 1 else per_dp // 2), per_dp // 2)
            sem = 2 * hop + (0 if k == 1 else 1)
            remote(
                inv.at[rows], inv.at[rows], x_send.at[0, sem], x_recv.at[0, sem], x_peer(lax.rem(k + nx, nx))
            ).wait_recv()

    inv_send(0)

    def rotate_g(slot):
        rows = pl.ds(pl.multiple_of(source(slot) * n_out, n_out), n_out)
        return contract_rows(bo[rows, :], g_buf[slot])

    def rotate_a(slot):
        rows = pl.ds(pl.multiple_of(source(slot) * n_in, n_in), n_in)
        return contract_rows(bi[rows, :], a_buf[slot])

    for copy in locals_[3:]:
        copy.wait()
    g_acc[...] = rotate_g(0)
    a_acc[...] = rotate_a(0)
    x_acc[...] = jnp.zeros_like(x_acc)
    norm_acc[...] = jnp.zeros_like(norm_acc)

    def stack(ref, width, n):
        pieces = []
        for slot in range(nz):
            at = pl.multiple_of(source(slot) * width + dp * n, n)
            pieces.append(ref[pl.ds(at, n), :])
        return jnp.concatenate(pieces, axis=0)

    def gq_copy(k):
        rows = pl.ds(pl.multiple_of(lax.rem(dp + k, nx) * q_out, q_out), q_out)
        return remote(gq_part.at[rows], gq_recv.at[k - 1], x_send.at[1, k - 1], x_recv.at[1, k - 1], x_peer(k))

    def aq_copy(k):
        return remote(aq_part, aq_recv.at[k - 1], x_send.at[2, k - 1], x_recv.at[2, k - 1], x_peer(k))

    def query_sums():
        gq_ring.take(stages, True)
        gq_part[...] = contract_rows(stack(bo, n_out, q_out), gq_buf[...].reshape(nz * q_out, n_c))
        for k in range(1, nx):
            gq_copy(k).start()

    def query_sums_in():
        aq_ring.end()
        aq_part[...] = contract_rows(stack(bi, n_in, q_in), aq_buf[...].reshape(nz * q_in, n_c))
        for k in range(1, nx):
            aq_copy(k).start()

    def rgq_copy(slot, k, theirs=False):
        rows = pl.ds(pl.multiple_of(lax.rem(dp + nx - k, nx) * q_out, q_out), q_out) if theirs else my_rows
        ref = rgq_buf.at[slot, rows]
        return remote(ref, ref, xg_send.at[slot, k - 1], xg_recv.at[slot, k - 1], x_peer(k))

    def gather(slot):
        for k in range(1, nx):
            rgq_copy(slot, k).start()

    def gathered(slot):
        for k in range(1, nx):
            rgq_copy(slot, k, theirs=True).wait_recv()

    def query_rotations():
        for k in range(1, nx):
            gq_copy(k).wait_recv()
        rgq_buf[0, my_rows] = (gq_part[my_rows] + gq_recv[0] + gq_recv[1] + gq_recv[2]).astype(BF16)
        rgq_ring.begin()
        gather(0)

    def query_rotations_in():
        for k in range(1, nx):
            aq_copy(k).wait_recv()
        rot_aq = (aq_part[...] + aq_recv[0] + aq_recv[1] + aq_recv[2]).astype(BF16).astype(F32)
        column = lax.broadcasted_iota(jnp.int32, (n_in, n_c), 1)
        for q in range(NQ):
            aq_mask[q * n_in:(q + 1) * n_in, :] = jnp.where(column // QSTEPS == q, rot_aq, 0.0).astype(BF16)

    def first_body(hop, c):
        @pl.when(hop < stages - 1)
        def _():
            gq_ring.relay(hop, False)

        @pl.when(hop == stages - 1)
        def _():
            gq_ring.relay(stages - 1, True)

        for ring in g_rings:
            ring.at(hop)

        aq_ring.at(hop)

        @pl.when(hop == stages - 1)
        def _():
            inv_take(0)
            inv_send(1)

        pl.when(hop == Q_SUM)(query_sums)
        pl.when(hop == Q_ROT)(query_rotations)

        @pl.when(hop > Q_ROT)
        def _():
            rgq_ring.relay(hop - Q_ROT)
            gather(hop - Q_ROT)
            gather(nz - hop + Q_ROT)

        pl.when(hop == A_LEAD)(a_rings[0].begin)
        pl.when(hop > A_LEAD)(lambda: a_rings[0].relay(hop - A_LEAD))

        g_acc[...] += rotate_g(hop) + rotate_g(nz - hop)
        return c

    lax.fori_loop(1, half, first_body, 0)
    for ring in a_rings[1:]:
        ring.begin()
    for ring in g_rings:
        ring.end()
    rg_buf[0] = (g_acc[...] + rotate_g(half)).astype(BF16)
    for ring in rg_rings:
        ring.begin()
    a_rings[0].relay(half - A_LEAD)
    early = half - Q_ROT
    rgq_ring.relay(early)
    gather(early)
    gather(nz - early)
    query_sums_in()
    inv_take(1)

    group = 2

    def score_block(slot):
        block_inv = inv[source(slot)]
        queries = rgq_buf[slot]
        train = rg_buf[slot]
        for part in range(NQ // group):
            rows = pl.ds(part * group * n_in, group * n_in)
            grad = lax.dot_general(
                aq_mask[rows, :], queries, (((1,), (1,)), ((), ())), preferred_element_type=F32
            ).reshape(group, n_in, n_out)
            precond = grad * block_inv[None]
            terms = (grad * precond).reshape(group, n_in // 8, 8, n_out).sum(axis=1)
            for lane in range(n_out // 128):
                norm_acc[part * group:(part + 1) * group] += terms[:, :, lane * 128:(lane + 1) * 128]
            x_acc[rows, :] += jnp.dot(
                precond.astype(BF16).reshape(group * n_in, n_out), train, preferred_element_type=F32
            )

    def second_body(hop, c):
        for ring in rg_rings:
            ring.at(hop)

        pl.when(hop <= A_LEAD)(lambda: a_rings[0].at(hop + half - A_LEAD))
        for ring in a_rings[1:]:
            ring.at(hop)

        @pl.when(hop <= Q_ROT)
        def _():
            rgq_ring.at(hop + early)

        @pl.when(hop < Q_ROT)
        def _():
            gather(hop + early)
            gather(nz - hop - early)

        pl.when(hop == Q_ROT)(lambda: gather(half))

        @pl.when(hop == 2)
        def _():
            query_rotations_in()
            for slot in (0, 1, nz - 1):
                gathered(slot)
            score_block(0)

        @pl.when((hop > 1) & (hop < half))
        def _():
            gathered(hop)
            gathered(nz - hop)

        pl.when(hop == half)(lambda: gathered(half))

        def blocks(i, c):
            slot = jnp.where(i == 0, hop, jnp.where(i == 1, nz - hop, jnp.where(i == 2, 1, nz - 1)))
            score_block(slot)
            return c

        lax.fori_loop(0, jnp.where(hop == 1, 0, jnp.where(hop == half, 1, jnp.where(hop == 2, 4, 2))), blocks, 0)

        def inputs(i, c):
            slot = jnp.where(i == 0, hop, nz - hop)
            a_acc[...] += rotate_a(slot)
            return c

        lax.fori_loop(0, jnp.where(hop == half, 1, 2), inputs, 0)
        return c

    lax.fori_loop(1, half + 1, second_body, 0)

    rot_a = a_acc[...].astype(BF16).astype(F32)
    for q in range(NQ):
        g_acc[q:q + 1, :] = jnp.sum(x_acc[q * n_in:(q + 1) * n_in, :] * rot_a, axis=0, keepdims=True)
    n_e = n_t // STEPS
    step_of = lax.broadcasted_iota(jnp.int32, (n_t, 128), 0) // STEPS
    lane = lax.broadcasted_iota(jnp.int32, (n_t, 128), 1)
    pick = jnp.where(step_of == lane % n_e, 1.0, 0.0)
    scores = jnp.dot(
        g_acc[0:NQ, :], pick, preferred_element_type=F32, precision=lax.Precision.HIGHEST
    )
    norms = jnp.sum(jnp.sum(norm_acc[...], axis=1), axis=1, keepdims=True)
    query = lax.broadcasted_iota(jnp.int32, (NQ, 128), 0)
    mine = lax.broadcasted_iota(jnp.int32, (NQ, 128), 1) // n_e == query
    msg[0:1, :] = jnp.sum(jnp.where(mine, scores, 0.0), axis=0, keepdims=True)
    msg[1:2, :] = jnp.sum(jnp.where(mine, norms, 0.0), axis=0, keepdims=True)

    def sum_copy(k):
        return remote(msg, sums.at[k - 1], z_send.at[k - 1], z_recv.at[k - 1], z_peer(k))

    order = sorted(range(1, nz), key=lambda k: -min(k, nz - k))
    for k in order:
        sum_copy(k).start()

    for ring in (gq_ring, aq_ring, rgq_ring) + g_rings + rg_rings + a_rings:
        ring.sent()
    for hop in (0, 1):
        for k in (1, -1):
            inv_copy(k, hop).wait_send()
    for k in range(1, nx):
        gq_copy(k).wait_send()
        aq_copy(k).wait_send()

    def sent_body(slot, c):
        for k in range(1, nx):
            rgq_copy(slot, k).wait_send()
        return c

    lax.fori_loop(0, nz, sent_body, 0)
    total = msg[...]
    for k in range(1, nz):
        sum_copy(k).wait_recv()
        total += sums[k - 1]
    out_ref[...] = total[0:1, :] / jnp.sqrt(total[1:2, :] * QSTEPS)
    for k in range(1, nz):
        sum_copy(k).wait_send()


def shards(nz, nx, a_train, g_train, a_query, g_query, basis_in, basis_out, eigen):
    n_in, n_t = a_train.shape
    n_out = g_train.shape[0]
    n_c = a_query.shape[1]
    q_in, q_out = n_in // nx, n_out // nx
    vmem = pltpu.VMEM
    dma = pltpu.SemaphoreType.DMA
    total = pl.pallas_call(
        functools.partial(kernel, nz, nx, G_CUTS, A_CUTS),
        out_shape=jax.ShapeDtypeStruct((1, 128), F32),
        in_specs=[pl.BlockSpec(memory_space=pl.ANY)] * 7,
        out_specs=pl.BlockSpec(memory_space=vmem),
        scratch_shapes=[
            vmem((nz, n_out, n_t), BF16),
            vmem((nz, n_in, n_t), BF16),
            vmem((nz, q_out, n_c), BF16),
            vmem((nz, q_in, n_c), BF16),
            vmem((nz, n_out, n_t), BF16),
            vmem((nz, n_out, n_c), BF16),
            vmem(basis_out.shape, BF16),
            vmem(basis_in.shape, BF16),
            vmem(eigen.shape, F32),
            vmem((nz, n_in, n_out), F32),
            vmem((n_out, n_t), F32),
            vmem((n_in, n_t), F32),
            vmem((n_out, n_c), F32),
            vmem((nx - 1, q_out, n_c), F32),
            vmem((n_in, n_c), F32),
            vmem((nx - 1, n_in, n_c), F32),
            vmem((NQ * n_in, n_c), BF16),
            vmem((NQ * n_in, n_t), F32),
            vmem((NQ, 8, 128), F32),
            vmem((2, 128), F32),
            vmem((nz - 1, 2, 128), F32),
            dma((3 + 2 * G_CUTS + A_CUTS, 2, nz // 2)),
            dma((3 + 2 * G_CUTS + A_CUTS, 2, nz // 2)),
            dma((3, 4)),
            dma((3, 4)),
            dma((nz, nx - 1)),
            dma((nz, nx - 1)),
            dma((nz - 1,)),
            dma((nz - 1,)),
            dma((7,)),
        ],
        compiler_params=pltpu.CompilerParams(
            collective_id=0, has_side_effects=True, vmem_limit_bytes=56 * 2**20
        ),
    )(a_train, g_train, a_query, g_query, basis_in, basis_out, eigen)
    return total.reshape(NQ, n_t // STEPS)


def solution(mesh):
    in_specs = (
        P(("member", "block"), "dp"),
        P(("member", "block"), "dp"),
        P(("member", "block"), None),
        P(("member", "block"), None),
        P("member", "block"),
        P("member", "block"),
        P(("member", "block"), "dp"),
    )
    body = functools.partial(shards, mesh.shape["block"], mesh.shape["dp"])
    return jax.shard_map(body, mesh=mesh, in_specs=in_specs, out_specs=P("member", "dp"), check_vma=False)
```

```python
import functools

import jax
import jax.numpy as jnp
from jax import lax
from jax.experimental import pallas as pl
from jax.experimental.pallas import tpu as pltpu
from jax.sharding import PartitionSpec as P

STEPS = 16
NQ = 8
QSTEPS = 16
DAMPING = 0.05

A_LEADS = (5, 7)
Q_SUM = 4
Q_ROT = 6
G_CUTS = 4
A_CUTS = len(A_LEADS)

MESH = pl.DeviceIdType.MESH
BF16 = jnp.bfloat16
F32 = jnp.float32


def contract_rows(left, right):
    return lax.dot_general(left, right, (((0,), (0,)), ((), ())), preferred_element_type=F32)


def kernel(
    nz, nx, g_cuts, a_cuts,
    a_ref, g_ref, aq_ref, gq_ref, bi_ref, bo_ref, eig_ref,
    out_ref,
    g_buf, a_buf, gq_buf, aq_buf, rg_buf, rgq_buf, bo, bi, eig, inv,
    g_acc, a_acc, gq_part, gq_recv, aq_part, aq_recv, aq_mask, x_acc, norm_acc, msg, sums,
    ring_send, ring_recv, x_send, x_recv, xg_send, xg_recv, z_send, z_recv, local_sem,
):
    half = nz // 2
    stages = half // 2
    me = lax.axis_index("block")
    dp = lax.axis_index("dp")
    n_in, n_t = a_ref.shape
    n_out = g_ref.shape[0]
    n_c = aq_ref.shape[1]
    q_in, q_out = n_in // nx, n_out // nx
    per_dp = nz // nx
    my_rows = pl.ds(pl.multiple_of(dp * q_out, q_out), q_out)

    def z_peer(k):
        return {"block": lax.rem(me + (k + nz), nz)}

    def x_peer(k):
        return {"dp": lax.rem(dp + k, nx)}

    def source(slot):
        return lax.rem(me + nz - slot, nz)

    locals_ = [
        pltpu.make_async_copy(gq_ref.at[my_rows], gq_buf.at[0], local_sem.at[0]),
        pltpu.make_async_copy(aq_ref.at[pl.ds(pl.multiple_of(dp * q_in, q_in), q_in)], aq_buf.at[0], local_sem.at[1]),
        pltpu.make_async_copy(eig_ref, eig, local_sem.at[2]),
        pltpu.make_async_copy(g_ref, g_buf.at[0], local_sem.at[3]),
        pltpu.make_async_copy(bo_ref, bo, local_sem.at[4]),
        pltpu.make_async_copy(a_ref, a_buf.at[0], local_sem.at[5]),
        pltpu.make_async_copy(bi_ref, bi, local_sem.at[6]),
    ]
    for copy in locals_:
        copy.start()

    barrier = pltpu.get_barrier_semaphore()
    near = (1, 2, -1, -2)
    for k in near:
        pl.semaphore_signal(barrier, inc=1, device_id=z_peer(k), device_id_type=MESH)
    for k in range(1, nx):
        pl.semaphore_signal(barrier, inc=1, device_id=x_peer(k), device_id_type=MESH)

    def remote(src, dst, send_sem, recv_sem, device):
        return pltpu.make_async_remote_copy(
            src_ref=src, dst_ref=dst, send_sem=send_sem, recv_sem=recv_sem,
            device_id=device, device_id_type=MESH,
        )

    def extent(way, part, lo, size):
        if not part:
            return pl.ds(lo, size)
        return pl.ds(lo + way * (size // 2), size // 2)

    class Ring:
        def __init__(self, index, buf, first, lo, size):
            self.index, self.buf, self.first, self.lo, self.size = index, buf, first, lo, size

        def copy(self, way, hop, part, own=False):
            rows = extent(way, part, self.lo, self.size)
            src_slot, dst_slot = (hop, hop + 1) if way == 0 else (lax.rem(nz - hop, nz), nz - 1 - hop)
            src = self.first.at[rows] if own else self.buf.at[src_slot, rows]
            return remote(
                src, self.buf.at[dst_slot, rows], ring_send.at[self.index, way, hop],
                ring_recv.at[self.index, way, hop], z_peer(1 if way == 0 else -1),
            )

        def begin(self):
            for way in (0, 1):
                self.copy(way, 0, False, own=True).start()

        def relay(self, hop):
            for way in (0, 1):
                self.copy(way, hop - 1, False).wait_recv()
                self.copy(way, hop, False).start()

        def relay_last(self):
            for way in (0, 1):
                self.copy(way, half - 2, False).wait_recv()
                self.copy(way, half - 1, True).start()

        def end(self):
            for way in (0, 1):
                self.copy(way, half - 1, True).wait_recv()

        def at(self, hop):
            pl.when(hop < half - 1)(lambda: self.relay(hop))
            pl.when(hop == half - 1)(self.relay_last)
            pl.when(hop == half)(self.end)

        def sent(self):
            def body(hop, c):
                for way in (0, 1):
                    self.copy(way, hop, False).wait_send()
                return c

            lax.fori_loop(0, half - 1, body, 0)
            for way in (0, 1):
                self.copy(way, half - 1, True).wait_send()

    class Stride:
        def __init__(self, index, buf, lo, size):
            self.index, self.buf, self.lo, self.size = index, buf, lo, size

        def copy(self, way, stage, ahead, part=False):
            rows = extent(way, part, self.lo, self.size)
            base = 2 * (stage - 1)
            src_slot, dst_slot = (base, base + ahead) if way == 0 else (lax.rem(nz - base, nz), nz - base - ahead)
            sem = base + ahead - 1
            return remote(
                self.buf.at[src_slot, rows], self.buf.at[dst_slot, rows], ring_send.at[self.index, way, sem],
                ring_recv.at[self.index, way, sem], z_peer(ahead if way == 0 else -ahead),
            )

        def send(self, stage, last=False):
            for way in (0, 1):
                self.copy(way, stage, 2, last).start()
            for way in (0, 1):
                self.copy(way, stage, 1).start()

        def take(self, stage, last=False):
            for way in (0, 1):
                self.copy(way, stage, 2, last).wait_recv()
            for way in (0, 1):
                self.copy(way, stage, 1).wait_recv()

        def relay(self, stage, last):
            for way in (0, 1):
                self.copy(way, stage, 2).wait_recv()
                self.copy(way, stage + 1, 2, last).start()
                self.copy(way, stage + 1, 1).start()
            for way in (0, 1):
                self.copy(way, stage, 1).wait_recv()

        def sent(self):
            for stage in range(1, stages + 1):
                for way in (0, 1):
                    self.copy(way, stage, 2, stage == stages).wait_send()
                    self.copy(way, stage, 1).wait_send()

    ho, hi = n_out // g_cuts, n_in // a_cuts
    gq_ring = Stride(0, gq_buf, 0, q_out)
    aq_ring = Ring(1, aq_buf, aq_buf.at[0], 0, q_in)
    rgq_ring = Ring(2, rgq_buf, rgq_buf.at[0], pl.multiple_of(dp * q_out, q_out), q_out)
    g_rings = tuple(Ring(3 + c, g_buf, g_ref, c * ho, ho) for c in range(g_cuts))
    rg_rings = tuple(Ring(3 + g_cuts + c, rg_buf, rg_buf.at[0], c * ho, ho) for c in range(g_cuts))
    a_rings = tuple(Ring(3 + 2 * g_cuts + c, a_buf, a_ref, c * hi, hi) for c in range(a_cuts))

    locals_[0].wait()
    locals_[1].wait()
    pl.semaphore_wait(barrier, len(near) + nx - 1)

    gq_ring.send(1)
    for ring in g_rings:
        ring.begin()
    aq_ring.begin()

    locals_[2].wait()
    for k in range(per_dp):
        inv[dp * per_dp + k] = 1.0 / (eig[:, k * n_out:(k + 1) * n_out] + DAMPING)

    def inv_copy(k, hop):
        owner = lax.rem(dp + nx - k * hop, nx)
        if hop == 0:
            rows = pl.ds(owner * per_dp, per_dp)
        else:
            rows = pl.ds(owner * per_dp + (0 if k == 1 else per_dp // 2), per_dp // 2)
        sem = 2 * hop + (0 if k == 1 else 1)
        return remote(inv.at[rows], inv.at[rows], x_send.at[0, sem], x_recv.at[0, sem], x_peer(lax.rem(k + nx, nx)))

    def inv_send(hop):
        for k in (1, -1):
            inv_copy(k, hop).start()

    def inv_take(hop):
        for k in (1, -1):
            owner = lax.rem(dp + nx - k * (hop + 1), nx)
            if hop == 0:
                rows = pl.ds(owner * per_dp, per_dp)
            else:
                rows = pl.ds(owner * per_dp + (0 if k == 1 else per_dp // 2), per_dp // 2)
            sem = 2 * hop + (0 if k == 1 else 1)
            remote(
                inv.at[rows], inv.at[rows], x_send.at[0, sem], x_recv.at[0, sem], x_peer(lax.rem(k + nx, nx))
            ).wait_recv()

    inv_send(0)

    def rotate_g(slot):
        rows = pl.ds(pl.multiple_of(source(slot) * n_out, n_out), n_out)
        return contract_rows(bo[rows, :], g_buf[slot])

    def rotate_a(slot):
        rows = pl.ds(pl.multiple_of(source(slot) * n_in, n_in), n_in)
        return contract_rows(bi[rows, :], a_buf[slot])

    for copy in locals_[3:]:
        copy.wait()
    g_acc[...] = rotate_g(0)
    a_acc[...] = rotate_a(0)
    x_acc[...] = jnp.zeros_like(x_acc)
    norm_acc[...] = jnp.zeros_like(norm_acc)

    def stack(ref, width, n):
        pieces = []
        for slot in range(nz):
            at = pl.multiple_of(source(slot) * width + dp * n, n)
            pieces.append(ref[pl.ds(at, n), :])
        return jnp.concatenate(pieces, axis=0)

    def gq_copy(k):
        rows = pl.ds(pl.multiple_of(lax.rem(dp + k, nx) * q_out, q_out), q_out)
        return remote(gq_part.at[rows], gq_recv.at[k - 1], x_send.at[1, k - 1], x_recv.at[1, k - 1], x_peer(k))

    def aq_copy(k):
        return remote(aq_part, aq_recv.at[k - 1], x_send.at[2, k - 1], x_recv.at[2, k - 1], x_peer(k))

    def query_sums():
        gq_ring.take(stages, True)
        gq_part[...] = contract_rows(stack(bo, n_out, q_out), gq_buf[...].reshape(nz * q_out, n_c))
        for k in range(1, nx):
            gq_copy(k).start()

    def query_sums_in():
        aq_ring.end()
        aq_part[...] = contract_rows(stack(bi, n_in, q_in), aq_buf[...].reshape(nz * q_in, n_c))
        for k in range(1, nx):
            aq_copy(k).start()

    def rgq_copy(slot, k, theirs=False):
        rows = pl.ds(pl.multiple_of(lax.rem(dp + nx - k, nx) * q_out, q_out), q_out) if theirs else my_rows
        ref = rgq_buf.at[slot, rows]
        return remote(ref, ref, xg_send.at[slot, k - 1], xg_recv.at[slot, k - 1], x_peer(k))

    def gather(slot):
        for k in range(1, nx):
            rgq_copy(slot, k).start()

    def gathered(slot):
        for k in range(1, nx):
            rgq_copy(slot, k, theirs=True).wait_recv()

    def query_rotations():
        for k in range(1, nx):
            gq_copy(k).wait_recv()
        rgq_buf[0, my_rows] = (gq_part[my_rows] + gq_recv[0] + gq_recv[1] + gq_recv[2]).astype(BF16)
        rgq_ring.begin()
        gather(0)

    def query_rotations_in():
        for k in range(1, nx):
            aq_copy(k).wait_recv()
        rot_aq = (aq_part[...] + aq_recv[0] + aq_recv[1] + aq_recv[2]).astype(BF16).astype(F32)
        column = lax.broadcasted_iota(jnp.int32, (n_in, n_c), 1)
        for q in range(NQ):
            aq_mask[q * n_in:(q + 1) * n_in, :] = jnp.where(column // QSTEPS == q, rot_aq, 0.0).astype(BF16)

    def first_body(hop, c):
        @pl.when(hop < stages - 1)
        def _():
            gq_ring.relay(hop, False)

        @pl.when(hop == stages - 1)
        def _():
            gq_ring.relay(stages - 1, True)

        for ring in g_rings:
            ring.at(hop)

        aq_ring.at(hop)

        @pl.when(hop == stages - 1)
        def _():
            inv_take(0)
            inv_send(1)

        pl.when(hop == Q_SUM)(query_sums)
        pl.when(hop == Q_ROT)(query_rotations)

        @pl.when(hop > Q_ROT)
        def _():
            rgq_ring.relay(hop - Q_ROT)
            gather(hop - Q_ROT)
            gather(nz - hop + Q_ROT)

        for lead, ring in zip(A_LEADS, a_rings):
            pl.when(hop == lead)(ring.begin)
            pl.when(hop > lead)(functools.partial(lambda one, by: one.relay(hop - by), ring, lead))

        g_acc[...] += rotate_g(hop) + rotate_g(nz - hop)
        return c

    lax.fori_loop(1, half, first_body, 0)
    for ring in g_rings:
        ring.end()
    rg_buf[0] = (g_acc[...] + rotate_g(half)).astype(BF16)
    for ring in rg_rings:
        ring.begin()
    for lead, ring in zip(A_LEADS, a_rings):
        ring.at(half - lead)
    early = half - Q_ROT
    rgq_ring.relay(early)
    gather(early)
    gather(nz - early)
    query_sums_in()
    inv_take(1)

    group = 2

    def score_block(slot):
        block_inv = inv[source(slot)]
        queries = rgq_buf[slot]
        train = rg_buf[slot]
        for part in range(NQ // group):
            rows = pl.ds(part * group * n_in, group * n_in)
            grad = lax.dot_general(
                aq_mask[rows, :], queries, (((1,), (1,)), ((), ())), preferred_element_type=F32
            ).reshape(group, n_in, n_out)
            precond = grad * block_inv[None]
            terms = (grad * precond).reshape(group, n_in // 8, 8, n_out).sum(axis=1)
            for lane in range(n_out // 128):
                norm_acc[part * group:(part + 1) * group] += terms[:, :, lane * 128:(lane + 1) * 128]
            x_acc[rows, :] += jnp.dot(
                precond.astype(BF16).reshape(group * n_in, n_out), train, preferred_element_type=F32
            )

    def second_body(hop, c):
        def inputs(i, c):
            slot = jnp.where(i == 0, hop, nz - hop)
            a_acc[...] += rotate_a(slot)
            return c

        lax.fori_loop(0, jnp.where(hop == half, 1, 2), inputs, 0)

        for ring in rg_rings:
            ring.at(hop)

        for lead, ring in zip(A_LEADS, a_rings):
            pl.when(hop <= lead)(functools.partial(lambda one, by: one.at(hop + half - by), ring, lead))

        @pl.when(hop <= Q_ROT)
        def _():
            rgq_ring.at(hop + early)

        @pl.when(hop < Q_ROT)
        def _():
            gather(hop + early)
            gather(nz - hop - early)

        pl.when(hop == Q_ROT)(lambda: gather(half))

        @pl.when(hop == 2)
        def _():
            query_rotations_in()
            for slot in (0, 1, nz - 1):
                gathered(slot)
            score_block(0)

        @pl.when((hop > 1) & (hop < half))
        def _():
            gathered(hop)
            gathered(nz - hop)

        pl.when(hop == half)(lambda: gathered(half))

        def blocks(i, c):
            slot = jnp.where(i == 0, hop, jnp.where(i == 1, nz - hop, jnp.where(i == 2, 1, nz - 1)))
            score_block(slot)
            return c

        lax.fori_loop(0, jnp.where(hop == 1, 0, jnp.where(hop == half, 1, jnp.where(hop == 2, 4, 2))), blocks, 0)

        return c

    lax.fori_loop(1, half + 1, second_body, 0)

    rot_a = a_acc[...].astype(BF16).astype(F32)
    for q in range(NQ):
        g_acc[q:q + 1, :] = jnp.sum(x_acc[q * n_in:(q + 1) * n_in, :] * rot_a, axis=0, keepdims=True)
    n_e = n_t // STEPS
    step_of = lax.broadcasted_iota(jnp.int32, (n_t, 128), 0) // STEPS
    lane = lax.broadcasted_iota(jnp.int32, (n_t, 128), 1)
    pick = jnp.where(step_of == lane % n_e, 1.0, 0.0)
    scores = jnp.dot(
        g_acc[0:NQ, :], pick, preferred_element_type=F32, precision=lax.Precision.HIGHEST
    )
    norms = jnp.sum(jnp.sum(norm_acc[...], axis=1), axis=1, keepdims=True)
    query = lax.broadcasted_iota(jnp.int32, (NQ, 128), 0)
    mine = lax.broadcasted_iota(jnp.int32, (NQ, 128), 1) // n_e == query
    msg[0:1, :] = jnp.sum(jnp.where(mine, scores, 0.0), axis=0, keepdims=True)
    msg[1:2, :] = jnp.sum(jnp.where(mine, norms, 0.0), axis=0, keepdims=True)

    def sum_copy(k):
        return remote(msg, sums.at[k - 1], z_send.at[k - 1], z_recv.at[k - 1], z_peer(k))

    order = sorted(range(1, nz), key=lambda k: -min(k, nz - k))
    for k in order:
        sum_copy(k).start()

    for ring in (gq_ring, aq_ring, rgq_ring) + g_rings + rg_rings + a_rings:
        ring.sent()
    for hop in (0, 1):
        for k in (1, -1):
            inv_copy(k, hop).wait_send()
    for k in range(1, nx):
        gq_copy(k).wait_send()
        aq_copy(k).wait_send()

    def sent_body(slot, c):
        for k in range(1, nx):
            rgq_copy(slot, k).wait_send()
        return c

    lax.fori_loop(0, nz, sent_body, 0)
    total = msg[...]
    for k in range(1, nz):
        sum_copy(k).wait_recv()
        total += sums[k - 1]
    out_ref[...] = total[0:1, :] / jnp.sqrt(total[1:2, :] * QSTEPS)
    for k in range(1, nz):
        sum_copy(k).wait_send()


def shards(nz, nx, a_train, g_train, a_query, g_query, basis_in, basis_out, eigen):
    n_in, n_t = a_train.shape
    n_out = g_train.shape[0]
    n_c = a_query.shape[1]
    q_in, q_out = n_in // nx, n_out // nx
    vmem = pltpu.VMEM
    dma = pltpu.SemaphoreType.DMA
    total = pl.pallas_call(
        functools.partial(kernel, nz, nx, G_CUTS, A_CUTS),
        out_shape=jax.ShapeDtypeStruct((1, 128), F32),
        in_specs=[pl.BlockSpec(memory_space=pl.ANY)] * 7,
        out_specs=pl.BlockSpec(memory_space=vmem),
        scratch_shapes=[
            vmem((nz, n_out, n_t), BF16),
            vmem((nz, n_in, n_t), BF16),
            vmem((nz, q_out, n_c), BF16),
            vmem((nz, q_in, n_c), BF16),
            vmem((nz, n_out, n_t), BF16),
            vmem((nz, n_out, n_c), BF16),
            vmem(basis_out.shape, BF16),
            vmem(basis_in.shape, BF16),
            vmem(eigen.shape, F32),
            vmem((nz, n_in, n_out), F32),
            vmem((n_out, n_t), F32),
            vmem((n_in, n_t), F32),
            vmem((n_out, n_c), F32),
            vmem((nx - 1, q_out, n_c), F32),
            vmem((n_in, n_c), F32),
            vmem((nx - 1, n_in, n_c), F32),
            vmem((NQ * n_in, n_c), BF16),
            vmem((NQ * n_in, n_t), F32),
            vmem((NQ, 8, 128), F32),
            vmem((2, 128), F32),
            vmem((nz - 1, 2, 128), F32),
            dma((3 + 2 * G_CUTS + A_CUTS, 2, nz // 2)),
            dma((3 + 2 * G_CUTS + A_CUTS, 2, nz // 2)),
            dma((3, 4)),
            dma((3, 4)),
            dma((nz, nx - 1)),
            dma((nz, nx - 1)),
            dma((nz - 1,)),
            dma((nz - 1,)),
            dma((7,)),
        ],
        compiler_params=pltpu.CompilerParams(
            collective_id=0, has_side_effects=True, vmem_limit_bytes=56 * 2**20
        ),
    )(a_train, g_train, a_query, g_query, basis_in, basis_out, eigen)
    return total.reshape(NQ, n_t // STEPS)


def solution(mesh):
    in_specs = (
        P(("member", "block"), "dp"),
        P(("member", "block"), "dp"),
        P(("member", "block"), None),
        P(("member", "block"), None),
        P("member", "block"),
        P("member", "block"),
        P(("member", "block"), "dp"),
    )
    body = functools.partial(shards, mesh.shape["block"], mesh.shape["dp"])
    return jax.shard_map(body, mesh=mesh, in_specs=in_specs, out_specs=P("member", "dp"), check_vma=False)
```
